512 devices in a mesh: ka: 64 (over z, y), row: 8 (over x, core).
Axes of the slice: x: 4, y: 4, z: 16, core: 2. Of those that a mesh axis runs over, the one named last changes fastest.
Arguments:
- inputs: bfloat16 [256, 16384], P(None, 'ka'), may hold values from -16 to 16
- weight: bfloat16 [18432, 16384], P('row', 'ka'), as said below
- out_grad: bfloat16 [256, 18432], P('ka', 'row'), may hold values from -16 to 16
Outputs:
- projected: bfloat16 [256, 18432], P('ka', 'row')
- input_grad: bfloat16 [256, 16384], P('row', 'ka')
- weight_grad: bfloat16 [18432, 16384], P('row', 'ka')
The draws below stay inside these ranges and needn't reach their ends.
Inputs may be any that keep to these rules, and one draw needn't show every extreme that they name: Every entry is finite and no row of the weight is all zero.
All inputs are finite; a program needn't handle non-finite values.
Results may differ from the reference program's by a relative error of at most 0.0049.
Values may be sent and summed in bfloat16 or wider, within the bound.
A program may use at most 64 MiB of HBM per device.

```python
import math
import jax
import jax.numpy as jnp
from jax import lax

D_IN = 16384
D_OUT = 18432
TOKENS = 256
LEVELS = 7


def draw_weight(key, part):
    key = jax.random.fold_in(key, 7)
    key_base, key_rows, key_cols = jax.random.split(key, 3)
    base = jnp.clip(jax.random.normal(key_base, (D_OUT, D_IN), jnp.float32), -5.0, 5.0)
    rows = jnp.exp(jax.random.uniform(key_rows, (D_OUT, 1), jnp.float32, jnp.log(0.5), jnp.log(2.0)))
    cols = jnp.exp(jax.random.uniform(key_cols, (1, D_IN), jnp.float32, jnp.log(0.3), jnp.log(3.0)))
    values = base * rows * cols * (1.0 / jnp.sqrt(jnp.float32(D_IN)))
    return values.astype(jnp.bfloat16)


def with_spikes(array, stream_key, source, target, shards_of, factor):
    owner, partner = [(jnp.arange(array.shape[dim]) // (array.shape[dim] // shards_of)).reshape([-1 if axis == dim else 1 for axis in range(array.ndim)]) for dim in (source, target)]
    chosen = jax.random.permutation(stream_key, shards_of)[partner]
    strong = (owner == chosen) | (owner == (partner + shards_of // 2) % shards_of)
    return jnp.where(strong, factor * array, array)


def shard_levels(stream_key, extent, cuts, low, largest):
    level = 1.0
    for position, blocks in cuts:
        heights = jax.random.uniform(jax.random.fold_in(jax.random.fold_in(stream_key, 6), position), (blocks,), jnp.float32, low / len(cuts), largest / len(cuts))
        level = level * jnp.repeat(jnp.exp(heights), extent[position] // blocks).reshape((-1,) + (1,) * (len(extent) - 1 - position))
    return level


def noise_with(key, extent, deviation, bound, cuts, heavy, dtype=jnp.bfloat16):
    entries = deviation * jax.random.normal(key, extent, jnp.float32)
    if cuts:
        entries = entries * shard_levels(key, extent, cuts, -0.22, 0.18)
    return jnp.clip(with_spikes(entries, jax.random.fold_in(key, 3), *heavy), -bound, bound).astype(dtype)


def setup_inputs(seed: int = 0) -> dict:
    splits = jax.random.split(jax.random.key(seed), 4)
    inputs = noise_with(splits[0], (TOKENS, D_IN), 1.0, 16.0, ((1, 64),), (1, 0, 64, 4.0))
    weight = draw_weight(jax.random.fold_in(splits[3], 71), 0)
    out_grad = noise_with(splits[2], (TOKENS, D_OUT), 1.0, 16.0, ((0, 64), (1, 8)), (1, 0, 64, 4.0))
    return {"inputs": inputs, "weight": weight, "out_grad": out_grad}


def quantize(weight):
    wide = weight.astype(jnp.float32)
    peak = lax.optimization_barrier(jnp.max(jnp.abs(wide), axis=1, keepdims=True))
    step = peak / LEVELS
    smooth = wide - step / (2.0 * math.pi) * jnp.sin(2.0 * math.pi * wide / step)
    return smooth.astype(jnp.bfloat16)

def reference(inputs, weight, out_grad):
    quantized = quantize(weight)
    projected = jnp.dot(inputs, quantized.T, preferred_element_type=jnp.float32).astype(jnp.bfloat16)
    input_grad = jnp.dot(out_grad, quantized, preferred_element_type=jnp.float32).astype(jnp.bfloat16)
    weight_grad = jnp.dot(out_grad.T, inputs, preferred_element_type=jnp.float32)
    weight_grad = (weight_grad * (1.0 / math.sqrt(TOKENS))).astype(jnp.bfloat16)
    return (projected, input_grad, weight_grad)
```

```python
import functools
import math

import jax
import jax.numpy as jnp
import numpy as np
from jax import lax
from jax.experimental import pallas as pl
from jax.experimental.pallas import tpu as pltpu
from jax.sharding import PartitionSpec as P

LEVELS = 7
MESH = pl.DeviceIdType.MESH
F32 = jnp.float32
BF16 = jnp.bfloat16

Z, Y, TOK = 16, 4, 4
CLASS = Z // 4
ROWS = 8
PIECES = (256, 512, 768, 768)

WINDOW = [(dy, dz) for dz in (2, 1, -1, 0) for dy in range(Y) if (dy, dz) != (0, 0)]
FAR = (8, 4, 12)
NEAR = (2, 1, 15)
AROUND = (8, 7, 9, 6, 10, 5, 11, 4, 12, 3, 13, 2, 14, 1, 15)


def sine_terms():
    nodes = 0.5 * np.cos((np.arange(4000) + 0.5) * np.pi / 8000)
    t = nodes * nodes
    basis = np.stack([t**k for k in range(7)], axis=1)
    scale = nodes[:, None]
    terms, *_ = np.linalg.lstsq(basis * scale, np.sin(2 * np.pi * nodes), rcond=None)
    return [float(c) for c in terms]


def quantized_block(wide, inverse, share, terms):
    turns = wide * inverse
    rest = turns - jnp.round(turns)
    square = rest * rest
    value = terms[-1] * square + terms[-2]
    for term in terms[-3::-1]:
        value = value * square + term
    return (wide - share * (rest * value)).astype(BF16)


def kernel(
    x_ref, w_ref, g_ref, projected_ref, input_ref, weight_ref,
    wt, qt, gathered, x_by_y, x_by_class, peak_own, peak_near, peak_mid, peak_far,
    part, part_in, sums, sums_in, grad, grad_in,
    near_s, near_r, far_s, far_r, g1_s, g1_r, g2_s, g2_r, g3_s, g3_r,
    part_s, part_r, sums_s, sums_r, grad_s, grad_r,
):
    ka, row = lax.axis_index("ka"), lax.axis_index("row")
    z, y = ka // Y, ka % Y
    low, high = z % 4, z // 4
    columns = w_ref.shape[0]
    terms = sine_terms()

    def at(dz, dy):
        return (lax.rem(z + dz + Z, Z) * Y + lax.rem(y + dy, Y), row)

    def beside(d):
        return (ka, lax.rem(row + d, ROWS))

    def send(source, target, sent, arrived, device):
        copy = pltpu.make_async_remote_copy(
            src_ref=source, dst_ref=target, send_sem=sent, recv_sem=arrived,
            device_id=device, device_id_type=MESH,
        )
        copy.start()
        return copy

    barrier = pltpu.get_barrier_semaphore()
    greeted = [at(dz, 0) for dz in AROUND if dz not in (1, 2, 15)]
    greeted += [at(-dz, dy) for dy, dz in WINDOW] + [beside(d) for d in range(1, ROWS)]
    for device in greeted:
        pl.semaphore_signal(barrier, inc=1, device_id=device, device_id_type=MESH)

    for c in range(0, columns, 256):
        wt[:, c : c + 256] = w_ref[c : c + 256, :].T
    peak_own[...] = jnp.max(jnp.abs(wt[...].astype(F32)), axis=0, keepdims=True)
    slot = low * 16 + high * Y + y
    gathered[slot] = g_ref[...]

    pl.semaphore_wait(barrier, len(greeted))

    near = [
        send(peak_own, peak_near.at[i], near_s.at[i], near_r.at[i], at(dz, dy))
        for i, (dy, dz) in enumerate(WINDOW)
    ]
    gather1 = [
        send(gathered.at[slot], gathered.at[slot], g1_s.at[i], g1_r.at[i], at(dz, 0))
        for i, dz in enumerate(FAR)
    ]

    to = lax.broadcasted_iota(jnp.int32, (256, 256), 0)
    come = lax.broadcasted_iota(jnp.int32, (256, 256), 1)
    order = jnp.where(come == to % 64 // TOK * 16 + to // 64 * TOK + to % TOK, 1.0, 0.0)
    x_by_y[...] = jnp.dot(order.astype(BF16), x_ref[...], preferred_element_type=F32).astype(BF16)
    for zh in range(4):
        for zl in range(4):
            x_by_class[64 * zl + 16 * zh : 64 * zl + 16 * zh + 16, :] = x_ref[
                64 * zh + 16 * zl : 64 * zh + 16 * zl + 16, :
            ]

    peak = peak_own[...]
    for i, copy in enumerate(near):
        copy.wait_recv()
        peak = jnp.maximum(peak, peak_near[i])
    peak_mid[...] = peak
    far = [
        send(peak_mid, peak_far.at[i], far_s.at[i], far_r.at[i], at(dz, 0))
        for i, dz in enumerate(FAR)
    ]

    for copy in gather1:
        copy.wait_recv()
    gather2 = []
    for dy in (2, 1, 3):
        for zh in range(4):
            i = len(gather2)
            held = gathered.at[low * 16 + zh * Y + y]
            gather2.append(send(held, held, g2_s.at[i], g2_r.at[i], at(0, dy)))

    for i, copy in enumerate(far):
        copy.wait_recv()
        peak = jnp.maximum(peak, peak_far[i])
    inverse = LEVELS / peak
    share = peak * (1.0 / (LEVELS * 2.0 * math.pi))

    starts = [sum(PIECES[:p]) for p in range(len(PIECES))]
    spans = [slice(s, s + n) for s, n in zip(starts, PIECES)]
    by_y, gather3 = [], []
    for p, span in enumerate(spans):
        for c in range(span.start, span.stop, 256):
            block = slice(c, c + 256)
            qt[:, block] = quantized_block(
                wt[:, block].astype(F32), inverse[:, block], share[:, block], terms
            )
            product = jnp.dot(x_by_y[...], qt[:, block], preferred_element_type=F32)
            part[:, :, block] = product.astype(BF16).reshape(Y, 64, 256)
        cut = pl.ds(span.start, PIECES[p])
        by_y.append([
            send(
                part.at[lax.rem(y + dy, Y), :, cut], part_in.at[i, :, cut],
                part_s.at[p, i], part_r.at[p, i], at(0, dy),
            )
            for i, dy in enumerate((2, 1, 3))
        ])
        if p == 0:
            for copy in gather2:
                copy.wait_recv()
            held = gathered.at[pl.ds(low * 16, 16)]
            gather3 = [
                send(held, held, g3_s.at[i], g3_r.at[i], at(dz, 0)) for i, dz in enumerate(NEAR)
            ]

    by_z = []
    for p, span in enumerate(spans):
        for copy in by_y[p]:
            copy.wait_recv()
        total = part[y, :, span].astype(F32)
        for i in range(3):
            total += part_in[i, :, span].astype(F32)
        for k in range(Z):
            sums[k, :, span] = total[TOK * k : TOK * k + TOK, :].astype(BF16)
        cut = pl.ds(span.start, PIECES[p])
        by_z.append([
            send(
                sums.at[lax.rem(z + dz, Z), :, cut], sums_in.at[i, :, cut],
                sums_s.at[p, i], sums_r.at[p, i], at(dz, 0),
            )
            for i, dz in enumerate(AROUND)
        ])

    for copy in gather3:
        copy.wait_recv()
    tokens = gathered[...].reshape(256, columns)
    product = lax.dot_general(
        tokens, qt[...], (((1,), (1,)), ((), ())), preferred_element_type=F32
    )
    for k in range(Z):
        start = 64 * (k % 4) + 16 * (k // 4)
        grad[k // 2, 16 * (k % 2) : 16 * (k % 2) + 16, :] = product[start : start + 16, :]
    by_row = [
        send(
            grad.at[lax.rem(row + d, ROWS)], grad_in.at[d - 1],
            grad_s.at[d - 1], grad_r.at[d - 1], beside(d),
        )
        for d in range(1, ROWS)
    ]

    for c in range(0, columns, 256):
        block = gathered[:, :, c : c + 256].reshape(256, 256)
        product = lax.dot_general(
            block, x_by_class[...], (((0,), (0,)), ((), ())), preferred_element_type=F32
        )
        weight_ref[c : c + 256, :] = (product * (1.0 / math.sqrt(x_ref.shape[0]))).astype(BF16)

    total = grad[row]
    for i, copy in enumerate(by_row):
        copy.wait_recv()
        total += grad_in[i]
    input_ref[...] = total.astype(BF16)

    for p, span in enumerate(spans):
        total = sums[z, :, span].astype(F32)
        for i, copy in enumerate(by_z[p]):
            copy.wait_recv()
            total += sums_in[i, :, span].astype(F32)
        projected_ref[:, span] = total.astype(BF16)

    for copy in near + far + gather1 + gather2 + gather3 + by_row + sum(by_y, []) + sum(by_z, []):
        copy.wait_send()


def local(inputs, weight, out_grad):
    columns, depth = weight.shape
    pieces = len(PIECES)
    whole = pl.BlockSpec(memory_space=pltpu.VMEM)
    dma = pltpu.SemaphoreType.DMA
    return pl.pallas_call(
        kernel,
        out_shape=(
            jax.ShapeDtypeStruct(out_grad.shape, BF16),
            jax.ShapeDtypeStruct((inputs.shape[0] // ROWS, depth), BF16),
            jax.ShapeDtypeStruct(weight.shape, BF16),
        ),
        in_specs=[whole] * 3,
        out_specs=(whole,) * 3,
        scratch_shapes=[
            pltpu.VMEM((depth, columns), BF16),
            pltpu.VMEM((depth, columns), BF16),
            pltpu.VMEM((Y * Z, TOK, columns), BF16),
            pltpu.VMEM(inputs.shape, BF16),
            pltpu.VMEM(inputs.shape, BF16),
            pltpu.VMEM((1, columns), F32),
            pltpu.VMEM((len(WINDOW), 1, columns), F32),
            pltpu.VMEM((1, columns), F32),
            pltpu.VMEM((len(FAR), 1, columns), F32),
            pltpu.VMEM((Y, Z * TOK, columns), BF16),
            pltpu.VMEM((Y - 1, Z * TOK, columns), BF16),
            pltpu.VMEM((Z, TOK, columns), BF16),
            pltpu.VMEM((Z - 1, TOK, columns), BF16),
            pltpu.VMEM((ROWS, inputs.shape[0] // ROWS, depth), F32),
            pltpu.VMEM((ROWS - 1, inputs.shape[0] // ROWS, depth), F32),
            dma((len(WINDOW),)), dma((len(WINDOW),)), dma((len(FAR),)), dma((len(FAR),)),
            dma((len(FAR),)), dma((len(FAR),)), dma((12,)), dma((12,)),
            dma((len(NEAR),)), dma((len(NEAR),)),
            dma((pieces, Y - 1)), dma((pieces, Y - 1)), dma((pieces, Z - 1)), dma((pieces, Z - 1)),
            dma((ROWS - 1,)), dma((ROWS - 1,)),
        ],
        compiler_params=pltpu.CompilerParams(
            collective_id=0, has_side_effects=True, vmem_limit_bytes=48 * 2**20
        ),
        name="joined_projection",
    )(inputs, weight, out_grad)


def solution(mesh):
    placed = (P(None, "ka"), P("row", "ka"), P("ka", "row"))
    return jax.shard_map(
        local,
        mesh=mesh,
        in_specs=placed,
        out_specs=(P("ka", "row"), P("row", "ka"), P("row", "ka")),
        check_vma=False,
    )
```

```python
import functools
import math

import jax
import jax.numpy as jnp
import numpy as np
from jax import lax
from jax.experimental import pallas as pl
from jax.experimental.pallas import tpu as pltpu
from jax.sharding import PartitionSpec as P

LEVELS = 7
MESH = pl.DeviceIdType.MESH
F32 = jnp.float32
BF16 = jnp.bfloat16

Z, Y, TOK = 16, 4, 4
CLASS = Z // 4
ROWS = 8
PIECES = (256, 512, 512, 512, 256, 256)
DIRECT = 2

WINDOW = [(dy, dz) for dz in (2, 1, -1, 0) for dy in range(Y) if (dy, dz) != (0, 0)]
FAR = (8, 4, 12)
NEAR = (2, 1, 15)
AROUND = (8, 7, 9, 6, 10, 5, 11, 4, 12, 3, 13, 2, 14, 1, 15)


def sine_terms():
    nodes = 0.5 * np.cos((np.arange(4000) + 0.5) * np.pi / 8000)
    t = nodes * nodes
    basis = np.stack([t**k for k in range(7)], axis=1)
    scale = nodes[:, None]
    terms, *_ = np.linalg.lstsq(basis * scale, np.sin(2 * np.pi * nodes), rcond=None)
    return [float(c) for c in terms]


def quantized_block(wide, inverse, share, terms):
    turns = wide * inverse
    rest = turns - jnp.round(turns)
    square = rest * rest
    value = terms[-1] * square + terms[-2]
    for term in terms[-3::-1]:
        value = value * square + term
    return (wide - share * (rest * value)).astype(BF16)


def kernel(
    x_hbm, w_hbm, g_hbm, projected_ref, input_ref, weight_ref,
    x_ref, w_ref, g_ref, load_sem, wt, qt, gathered, x_by_y, x_by_class, peak_own, peak_near, peak_mid, peak_far,
    part, part_in, sums, near_in, sums_far, sums_in, grad, grad_in,
    near_s, near_r, far_s, far_r, g1_s, g1_r, g2_s, g2_r, g3_s, g3_r,
    part_s, part_r, part_near_s, part_near_r, sums_s, sums_r, grad_s, grad_r,
):
    ka, row = lax.axis_index("ka"), lax.axis_index("row")
    z, y = ka // Y, ka % Y
    low, high = z % 4, z // 4
    columns = w_hbm.shape[0]
    terms = sine_terms()

    def at(dz, dy):
        return (lax.rem(z + dz + Z, Z) * Y + lax.rem(y + dy, Y), row)

    def beside(d):
        return (ka, lax.rem(row + d, ROWS))

    def send(source, target, sent, arrived, device):
        copy = pltpu.make_async_remote_copy(
            src_ref=source, dst_ref=target, send_sem=sent, recv_sem=arrived,
            device_id=device, device_id_type=MESH,
        )
        copy.start()
        return copy

    barrier = pltpu.get_barrier_semaphore()
    greeted = [at(dz, 0) for dz in AROUND if dz not in (1, 2, 15)]
    greeted += [at(-dz, dy) for dy, dz in WINDOW] + [beside(d) for d in range(1, ROWS)]
    for device in greeted:
        pl.semaphore_signal(barrier, inc=1, device_id=device, device_id_type=MESH)

    loads = [
        pltpu.make_async_copy(source, target, load_sem.at[i])
        for i, (source, target) in enumerate(((w_hbm, w_ref), (g_hbm, g_ref), (x_hbm, x_ref)))
    ]
    for copy in loads:
        copy.start()

    loads[0].wait()
    for c in range(0, columns, 256):
        wt[:, c : c + 256] = w_ref[c : c + 256, :].T
    peak_own[...] = jnp.max(jnp.abs(wt[...].astype(F32)), axis=0, keepdims=True)
    slot = low * 16 + y * CLASS + high
    loads[1].wait()
    loads[2].wait()
    gathered[slot] = g_ref[...]

    pl.semaphore_wait(barrier, len(greeted))

    near = [
        send(peak_own, peak_near.at[i], near_s.at[i], near_r.at[i], at(dz, dy))
        for i, (dy, dz) in enumerate(WINDOW)
    ]
    gather1 = [
        send(gathered.at[slot], gathered.at[slot], g1_s.at[i], g1_r.at[i], at(dz, 0))
        for i, dz in enumerate(FAR)
    ]

    to = lax.broadcasted_iota(jnp.int32, (256, 256), 0)
    come = lax.broadcasted_iota(jnp.int32, (256, 256), 1)
    by_y = to % 64 // TOK * 16 + to // 64 * TOK + to % TOK
    by_class = to // 64 * 16 + to // 16 % 4 * TOK + to // 4 % 4 * 64 + to % TOK
    for source, target in ((by_y, x_by_y), (by_class, x_by_class)):
        order = jnp.where(come == source, 1.0, 0.0).astype(BF16)
        target[...] = jnp.dot(order, x_ref[...], preferred_element_type=F32).astype(BF16)

    peak = peak_own[...]
    for i, copy in enumerate(near):
        copy.wait_recv()
        peak = jnp.maximum(peak, peak_near[i])
    peak_mid[...] = peak
    far = [
        send(peak_mid, peak_far.at[i], far_s.at[i], far_r.at[i], at(dz, 0))
        for i, dz in enumerate(FAR)
    ]

    for copy in gather1:
        copy.wait_recv()
    held = gathered.at[pl.ds(low * 16 + y * CLASS, CLASS)]
    gather2 = [
        send(held, held, g2_s.at[i], g2_r.at[i], device)
        for i, device in enumerate([at(dz, 0) for dz in NEAR] + [at(0, dy) for dy in (2, 1, 3)])
    ]

    for i, copy in enumerate(far):
        copy.wait_recv()
        peak = jnp.maximum(peak, peak_far[i])
    inverse = LEVELS / peak
    share = peak * (1.0 / (LEVELS * 2.0 * math.pi))

    starts = [sum(PIECES[:p]) for p in range(len(PIECES))]
    spans = [slice(s, s + n) for s, n in zip(starts, PIECES)]
    by_y, gather3 = [], []
    for p, span in enumerate(spans):
        for c in range(span.start, span.stop, 256):
            block = slice(c, c + 256)
            qt[:, block] = quantized_block(
                wt[:, block].astype(F32), inverse[:, block], share[:, block], terms
            )
            product = jnp.dot(x_by_y[...], qt[:, block], preferred_element_type=F32)
            part[:, :, block] = product.astype(BF16).reshape(Y, 64, 256)
        cut = pl.ds(span.start, PIECES[p])
        by_y.append([
            send(
                part.at[lax.rem(y + dy, Y), :, cut], part_in.at[i, :, cut],
                part_s.at[p, i], part_r.at[p, i], at(0, dy),
            )
            for i, dy in enumerate((2, 1, 3))
        ])
        if p == 0:
            for copy in gather2:
                copy.wait_recv()
            for dy in (2, 1, 3):
                first = low * 16 + lax.rem(y + dy, Y) * CLASS
                for dz, start, size in ((1, 0, 4), (15, 0, 4), (2, 0, 2), (14, 2, 2)):
                    i = len(gather3)
                    held = gathered.at[pl.ds(first + start, size)]
                    gather3.append(send(held, held, g3_s.at[i], g3_r.at[i], at(dz, 0)))

    def chunk(k):
        return lax.rem(k, 4) * CLASS + k // 4

    def near_total(p):
        span, cut = spans[p], pl.ds(spans[p].start, PIECES[p])
        for copy in by_near[p]:
            copy.wait_recv()
        total = sums[pl.ds(low * CLASS, CLASS), :, span].astype(F32)
        for i in range(3):
            total += near_in[i, :, :, span].astype(F32)
        sums_far[:, :, span] = total.astype(BF16)
        by_z[p] = [
            send(
                sums_far.at[lax.rem(high + m, CLASS), :, cut], sums_in.at[i, :, cut],
                sums_s.at[p, i], sums_r.at[p, i], at(4 * m, 0),
            )
            for i, m in enumerate((2, 1, 3))
        ]

    by_z, by_near = {}, {}
    for p, span in enumerate(spans):
        for copy in by_y[p]:
            copy.wait_recv()
        total = part[y, :, span].astype(F32)
        for i in range(3):
            total += part_in[i, :, span].astype(F32)
        for k in range(Z):
            sums[k % 4 * CLASS + k // 4, :, span] = total[TOK * k : TOK * k + TOK, :].astype(BF16)
        cut = pl.ds(span.start, PIECES[p])
        if p >= len(PIECES) - DIRECT:
            by_z[p] = [
                send(
                    sums.at[chunk(lax.rem(z + dz, Z)), :, cut], sums_in.at[i, :, cut],
                    sums_s.at[p, i], sums_r.at[p, i], at(dz, 0),
                )
                for i, dz in enumerate(AROUND)
            ]
        else:
            by_near[p] = [
                send(
                    sums.at[pl.ds(lax.rem(low + dz, 4) * CLASS + first, count), :, cut],
                    near_in.at[i, pl.ds(first, count), :, cut],
                    part_near_s.at[p, j], part_near_r.at[p, j], at(dz, 0),
                )
                for j, (i, dz, first, count) in enumerate(
                    ((0, 1, 0, 4), (1, 15, 0, 4), (2, 2, 0, 2), (2, 14, 2, 2))
                )
            ]
        if p >= 1 and p - 1 in by_near:
            near_total(p - 1)
    if not DIRECT:
        near_total(len(PIECES) - 1)

    for copy in gather3:
        copy.wait_recv()
    tokens = gathered[...].reshape(256, columns)
    product = lax.dot_general(
        tokens, qt[...], (((1,), (1,)), ((), ())), preferred_element_type=F32
    )
    for k in range(Y * Z):
        start = k // Y % 4 * 64 + k % Y * 16 + k // 16 * TOK
        grad[k // 8, k % 8 * TOK : k % 8 * TOK + TOK, :] = product[start : start + TOK, :]
    by_row = [
        send(
            grad.at[lax.rem(row + d, ROWS)], grad_in.at[d - 1],
            grad_s.at[d - 1], grad_r.at[d - 1], beside(d),
        )
        for d in range(1, ROWS)
    ]

    for c in range(0, columns, 256):
        block = gathered[:, :, c : c + 256].reshape(256, 256)
        product = lax.dot_general(
            block, x_by_class[...], (((0,), (0,)), ((), ())), preferred_element_type=F32
        )
        weight_ref[c : c + 256, :] = (product * (1.0 / math.sqrt(x_hbm.shape[0]))).astype(BF16)

    total = grad[row]
    for i, copy in enumerate(by_row):
        copy.wait_recv()
        total += grad_in[i]
    input_ref[...] = total.astype(BF16)

    for p, span in enumerate(spans):
        direct = p >= len(PIECES) - DIRECT
        total = (sums[chunk(z), :, span] if direct else sums_far[high, :, span]).astype(F32)
        for i, copy in enumerate(by_z[p]):
            copy.wait_recv()
            total += sums_in[i, :, span].astype(F32)
        projected_ref[:, span] = total.astype(BF16)

    for copy in near + far + gather1 + gather2 + gather3 + by_row + sum(by_y, []):
        copy.wait_send()
    for copy in sum(by_near.values(), []) + sum(by_z.values(), []):
        copy.wait_send()


def local(inputs, weight, out_grad):
    columns, depth = weight.shape
    pieces = len(PIECES)
    whole = pl.BlockSpec(memory_space=pltpu.VMEM)
    dma = pltpu.SemaphoreType.DMA
    return pl.pallas_call(
        kernel,
        out_shape=(
            jax.ShapeDtypeStruct(out_grad.shape, BF16),
            jax.ShapeDtypeStruct((inputs.shape[0] // ROWS, depth), BF16),
            jax.ShapeDtypeStruct(weight.shape, BF16),
        ),
        in_specs=[pl.BlockSpec(memory_space=pltpu.HBM)] * 3,
        out_specs=(whole,) * 3,
        scratch_shapes=[
            pltpu.VMEM(inputs.shape, BF16),
            pltpu.VMEM(weight.shape, BF16),
            pltpu.VMEM(out_grad.shape, BF16),
            dma((3,)),
            pltpu.VMEM((depth, columns), BF16),
            pltpu.VMEM((depth, columns), BF16),
            pltpu.VMEM((Y * Z, TOK, columns), BF16),
            pltpu.VMEM(inputs.shape, BF16),
            pltpu.VMEM(inputs.shape, BF16),
            pltpu.VMEM((1, columns), F32),
            pltpu.VMEM((len(WINDOW), 1, columns), F32),
            pltpu.VMEM((1, columns), F32),
            pltpu.VMEM((len(FAR), 1, columns), F32),
            pltpu.VMEM((Y, Z * TOK, columns), BF16),
            pltpu.VMEM((Y - 1, Z * TOK, columns), BF16),
            pltpu.VMEM((Z, TOK, columns), BF16),
            pltpu.VMEM((3, CLASS, TOK, columns), BF16),
            pltpu.VMEM((CLASS, TOK, columns), BF16),
            pltpu.VMEM((Z - 1, TOK, columns), BF16),
            pltpu.VMEM((ROWS, inputs.shape[0] // ROWS, depth), F32),
            pltpu.VMEM((ROWS - 1, inputs.shape[0] // ROWS, depth), F32),
            dma((len(WINDOW),)), dma((len(WINDOW),)), dma((len(FAR),)), dma((len(FAR),)),
            dma((len(FAR),)), dma((len(FAR),)), dma((6,)), dma((6,)), dma((12,)), dma((12,)),
            dma((pieces, Y - 1)), dma((pieces, Y - 1)), dma((pieces, 4)), dma((pieces, 4)),
            dma((pieces, Z - 1)), dma((pieces, Z - 1)),
            dma((ROWS - 1,)), dma((ROWS - 1,)),
        ],
        compiler_params=pltpu.CompilerParams(
            collective_id=0, has_side_effects=True, vmem_limit_bytes=int(52.4 * 2**20)
        ),
        name="joined_projection",
    )(inputs, weight, out_grad)


def solution(mesh):
    placed = (P(None, "ka"), P("row", "ka"), P("ka", "row"))
    return jax.shard_map(
        local,
        mesh=mesh,
        in_specs=placed,
        out_specs=(P("ka", "row"), P("row", "ka"), P("row", "ka")),
        check_vma=False,
    )
```

```python
import functools
import math

import jax
import jax.numpy as jnp
import numpy as np
from jax import lax
from jax.experimental import pallas as pl
from jax.experimental.pallas import tpu as pltpu
from jax.sharding import PartitionSpec as P

LEVELS = 7
MESH = pl.DeviceIdType.MESH
F32 = jnp.float32
BF16 = jnp.bfloat16

Z, Y, TOK = 16, 4, 4
CLASS = Z // 4
ROWS = 8
PIECES = (256, 512, 512, 512, 256, 256)
DIRECT = 4

WINDOW = [(dy, dz) for dz in (2, 1, -1, 0) for dy in range(Y) if (dy, dz) != (0, 0)]
FAR = (8, 4, 12)
NEAR = (2, 1, 15)
AROUND = (8, 7, 9, 6, 10, 5, 11, 4, 12, 3, 13, 2, 14, 1, 15)


def sine_terms():
    nodes = 0.5 * np.cos((np.arange(4000) + 0.5) * np.pi / 8000)
    t = nodes * nodes
    basis = np.stack([t**k for k in range(7)], axis=1)
    scale = nodes[:, None]
    terms, *_ = np.linalg.lstsq(basis * scale, np.sin(2 * np.pi * nodes), rcond=None)
    return [float(c) for c in terms]


def quantized_block(wide, inverse, share, terms):
    turns = wide * inverse
    rest = turns - jnp.round(turns)
    square = rest * rest
    value = terms[-1] * square + terms[-2]
    for term in terms[-3::-1]:
        value = value * square + term
    return (wide - share * (rest * value)).astype(BF16)


def kernel(
    x_hbm, w_hbm, g_hbm, projected_hbm, input_hbm, weight_hbm,
    projected_ref, input_ref, weight_ref, store_sem, x_ref, w_ref, g_ref, load_sem, wt, qt, gathered, x_by_y, x_by_class, peak_own, peak_near, peak_mid, peak_far,
    part, part_in, sums, near_in, sums_far, sums_in, grad, grad_in,
    near_s, near_r, far_s, far_r, g1_s, g1_r, g2_s, g2_r, g3_s, g3_r,
    part_s, part_r, part_near_s, part_near_r, sums_s, sums_r, grad_s, grad_r,
):
    ka, row = lax.axis_index("ka"), lax.axis_index("row")
    z, y = ka // Y, ka % Y
    low, high = z % 4, z // 4
    columns = w_hbm.shape[0]
    terms = sine_terms()

    def at(dz, dy):
        return (lax.rem(z + dz + Z, Z) * Y + lax.rem(y + dy, Y), row)

    def beside(d):
        return (ka, lax.rem(row + d, ROWS))

    def send(source, target, sent, arrived, device):
        copy = pltpu.make_async_remote_copy(
            src_ref=source, dst_ref=target, send_sem=sent, recv_sem=arrived,
            device_id=device, device_id_type=MESH,
        )
        copy.start()
        return copy

    barrier = pltpu.get_barrier_semaphore()
    greeted = [at(dz, 0) for dz in AROUND if dz not in (1, 2, 15)]
    greeted += [at(-dz, dy) for dy, dz in WINDOW] + [beside(d) for d in range(1, ROWS)]
    for device in greeted:
        pl.semaphore_signal(barrier, inc=1, device_id=device, device_id_type=MESH)

    loads = [
        pltpu.make_async_copy(source, target, load_sem.at[i])
        for i, (source, target) in enumerate(((w_hbm, w_ref), (g_hbm, g_ref), (x_hbm, x_ref)))
    ]
    for copy in loads:
        copy.start()

    loads[0].wait()
    for c in range(0, columns, 256):
        wt[:, c : c + 256] = w_ref[c : c + 256, :].T
    peak_own[...] = jnp.max(jnp.abs(wt[...].astype(F32)), axis=0, keepdims=True)
    slot = low * 16 + y * CLASS + high
    loads[1].wait()
    loads[2].wait()
    gathered[slot] = g_ref[...]

    pl.semaphore_wait(barrier, len(greeted))

    near = [
        send(peak_own, peak_near.at[i], near_s.at[i], near_r.at[i], at(dz, dy))
        for i, (dy, dz) in enumerate(WINDOW)
    ]
    gather1 = [
        send(gathered.at[slot], gathered.at[slot], g1_s.at[i], g1_r.at[i], at(dz, 0))
        for i, dz in enumerate(FAR)
    ]

    to = lax.broadcasted_iota(jnp.int32, (256, 256), 0)
    come = lax.broadcasted_iota(jnp.int32, (256, 256), 1)
    by_y = to % 64 // TOK * 16 + to // 64 * TOK + to % TOK
    by_class = to // 64 * 16 + to // 16 % 4 * TOK + to // 4 % 4 * 64 + to % TOK
    for source, target in ((by_y, x_by_y), (by_class, x_by_class)):
        order = jnp.where(come == source, 1.0, 0.0).astype(BF16)
        target[...] = jnp.dot(order, x_ref[...], preferred_element_type=F32).astype(BF16)

    peak = peak_own[...]
    for i, copy in enumerate(near):
        copy.wait_recv()
        peak = jnp.maximum(peak, peak_near[i])
    peak_mid[...] = peak
    far = [
        send(peak_mid, peak_far.at[i], far_s.at[i], far_r.at[i], at(dz, 0))
        for i, dz in enumerate(FAR)
    ]

    for copy in gather1:
        copy.wait_recv()
    held = gathered.at[pl.ds(low * 16 + y * CLASS, CLASS)]
    gather2 = [
        send(held, held, g2_s.at[i], g2_r.at[i], device)
        for i, device in enumerate([at(dz, 0) for dz in NEAR] + [at(0, dy) for dy in (2, 1, 3)])
    ]

    for i, copy in enumerate(far):
        copy.wait_recv()
        peak = jnp.maximum(peak, peak_far[i])
    inverse = LEVELS / peak
    share = peak * (1.0 / (LEVELS * 2.0 * math.pi))

    starts = [sum(PIECES[:p]) for p in range(len(PIECES))]
    spans = [slice(s, s + n) for s, n in zip(starts, PIECES)]
    by_y, gather3 = [], []
    for p, span in enumerate(spans):
        for c in range(span.start, span.stop, 256):
            block = slice(c, c + 256)
            qt[:, block] = quantized_block(
                wt[:, block].astype(F32), inverse[:, block], share[:, block], terms
            )
            product = jnp.dot(x_by_y[...], qt[:, block], preferred_element_type=F32)
            part[:, :, block] = product.astype(BF16).reshape(Y, 64, 256)
        cut = pl.ds(span.start, PIECES[p])
        by_y.append([
            send(
                part.at[lax.rem(y + dy, Y), :, cut], part_in.at[i, :, cut],
                part_s.at[p, i], part_r.at[p, i], at(0, dy),
            )
            for i, dy in enumerate((2, 1, 3))
        ])
        if p == 0:
            for copy in gather2:
                copy.wait_recv()
            for dy in (2, 1, 3):
                held_y = low * 16 + lax.rem(y + dy, Y) * CLASS
                for dz, start, size in ((1, 0, 3), (15, 0, 3), (2, 0, 2), (14, 2, 1)):
                    i = len(gather3)
                    held = gathered.at[pl.ds(held_y + start, size)]
                    gather3.append(send(held, held, g3_s.at[i], g3_r.at[i], at(dz, 0)))

    for dz in (1, 2, 3):
        held = gathered.at[pl.ds(lax.rem(low + dz, 4) * 16 + y * CLASS + 3, 1)]
        for dy in (2, 1, 3):
            i = len(gather3)
            gather3.append(send(held, held, g3_s.at[i], g3_r.at[i], at(0, dy)))

    def chunk(k):
        return lax.rem(k, 4) * CLASS + k // 4

    def near_total(p):
        span, cut = spans[p], pl.ds(spans[p].start, PIECES[p])
        for copy in by_near[p]:
            copy.wait_recv()
        total = sums[pl.ds(low * CLASS, CLASS), :, span].astype(F32)
        for i in range(3):
            total += near_in[i, :, :, span].astype(F32)
        sums_far[:, :, span] = total.astype(BF16)
        by_z[p] = [
            send(
                sums_far.at[lax.rem(high + m, CLASS), :, cut], sums_in.at[i, :, cut],
                sums_s.at[p, i], sums_r.at[p, i], at(4 * m, 0),
            )
            for i, m in enumerate((2, 1, 3))
        ]

    by_z, by_near = {}, {}
    for p, span in enumerate(spans):
        for copy in by_y[p]:
            copy.wait_recv()
        total = part[y, :, span].astype(F32)
        for i in range(3):
            total += part_in[i, :, span].astype(F32)
        for k in range(Z):
            sums[k % 4 * CLASS + k // 4, :, span] = total[TOK * k : TOK * k + TOK, :].astype(BF16)
        cut = pl.ds(span.start, PIECES[p])
        if p >= len(PIECES) - DIRECT:
            by_z[p] = [
                send(
                    sums.at[chunk(lax.rem(z + dz, Z)), :, cut], sums_in.at[i, :, cut],
                    sums_s.at[p, i], sums_r.at[p, i], at(dz, 0),
                )
                for i, dz in enumerate(AROUND)
            ]
        else:
            by_near[p] = [
                send(
                    sums.at[pl.ds(lax.rem(low + dz, 4) * CLASS + first, count), :, cut],
                    near_in.at[i, pl.ds(first, count), :, cut],
                    part_near_s.at[p, j], part_near_r.at[p, j], at(dz, 0),
                )
                for j, (i, dz, first, count) in enumerate(
                    ((0, 1, 0, 4), (1, 15, 0, 4), (2, 2, 0, 2), (2, 14, 2, 2))
                )
            ]
        if p >= 1 and p - 1 in by_near:
            near_total(p - 1)
    if not DIRECT:
        near_total(len(PIECES) - 1)

    for copy in gather3:
        copy.wait_recv()
    tokens = gathered[...].reshape(256, columns)
    product = lax.dot_general(
        tokens, qt[...], (((1,), (1,)), ((), ())), preferred_element_type=F32
    )
    for k in range(Y * Z):
        start = k // Y % 4 * 64 + k % Y * 16 + k // 16 * TOK
        grad[k // 8, k % 8 * TOK : k % 8 * TOK + TOK, :] = product[start : start + TOK, :]
    by_row = [
        send(
            grad.at[lax.rem(row + d, ROWS)], grad_in.at[d - 1],
            grad_s.at[d - 1], grad_r.at[d - 1], beside(d),
        )
        for d in range(1, ROWS)
    ]

    for c in range(0, columns, 256):
        block = gathered[:, :, c : c + 256].reshape(256, 256)
        product = lax.dot_general(
            block, x_by_class[...], (((0,), (0,)), ((), ())), preferred_element_type=F32
        )
        weight_ref[c : c + 256, :] = (product * (1.0 / math.sqrt(x_hbm.shape[0]))).astype(BF16)

    stores = [
        pltpu.make_async_copy(source, target, store_sem.at[i])
        for i, (source, target) in enumerate(
            ((weight_ref, weight_hbm), (input_ref, input_hbm), (projected_ref, projected_hbm))
        )
    ]
    stores[0].start()

    total = grad[row]
    for i, copy in enumerate(by_row):
        copy.wait_recv()
        total += grad_in[i]
    input_ref[...] = total.astype(BF16)
    stores[1].start()

    for p, span in enumerate(spans):
        direct = p >= len(PIECES) - DIRECT
        total = (sums[chunk(z), :, span] if direct else sums_far[high, :, span]).astype(F32)
        for i, copy in enumerate(by_z[p]):
            copy.wait_recv()
            total += sums_in[i, :, span].astype(F32)
        projected_ref[:, span] = total.astype(BF16)
    stores[2].start()

    for copy in near + far + gather1 + gather2 + gather3 + by_row + sum(by_y, []):
        copy.wait_send()
    for copy in sum(by_near.values(), []) + sum(by_z.values(), []):
        copy.wait_send()
    for copy in stores:
        copy.wait()


def hand_over(*refs):
    sources, targets, held, came, done = refs[:3], refs[3:6], refs[6:9], refs[9], refs[10]
    moves = []
    for source, target, here in zip(sources, targets, held):
        rows = source.shape[0]
        parts = 4 if rows >= 2048 else 1
        for k in range(parts):
            cut, i = pl.ds(k * (rows // parts), rows // parts), len(moves)
            moves.append((
                pltpu.make_async_copy(source.at[cut], here.at[cut], came.at[i]),
                pltpu.make_async_copy(here.at[cut], target.at[cut], done.at[i]),
            ))
    for come, _ in moves:
        come.start()
    for come, go in moves:
        come.wait()
        go.start()
    for _, go in moves:
        go.wait()


def local(inputs, weight, out_grad):
    columns, depth = weight.shape
    pieces = len(PIECES)
    anywhere = pl.BlockSpec(memory_space=pl.ANY)
    dma = pltpu.SemaphoreType.DMA
    results = pl.pallas_call(
        kernel,
        out_shape=(
            jax.ShapeDtypeStruct(out_grad.shape, BF16),
            jax.ShapeDtypeStruct((inputs.shape[0] // ROWS, depth), BF16),
            jax.ShapeDtypeStruct(weight.shape, BF16),
        ),
        in_specs=[anywhere] * 3,
        out_specs=(anywhere,) * 3,
        scratch_shapes=[
            pltpu.VMEM(out_grad.shape, BF16),
            pltpu.VMEM((inputs.shape[0] // ROWS, depth), BF16),
            pltpu.VMEM(weight.shape, BF16),
            dma((3,)),
            pltpu.VMEM(inputs.shape, BF16),
            pltpu.VMEM(weight.shape, BF16),
            pltpu.VMEM(out_grad.shape, BF16),
            dma((3,)),
            pltpu.VMEM((depth, columns), BF16),
            pltpu.VMEM((depth, columns), BF16),
            pltpu.VMEM((Y * Z, TOK, columns), BF16),
            pltpu.VMEM(inputs.shape, BF16),
            pltpu.VMEM(inputs.shape, BF16),
            pltpu.VMEM((1, columns), F32),
            pltpu.VMEM((len(WINDOW), 1, columns), F32),
            pltpu.VMEM((1, columns), F32),
            pltpu.VMEM((len(FAR), 1, columns), F32),
            pltpu.VMEM((Y, Z * TOK, columns), BF16),
            pltpu.VMEM((Y - 1, Z * TOK, columns), BF16),
            pltpu.VMEM((Z, TOK, columns), BF16),
            pltpu.VMEM((3, CLASS, TOK, columns), BF16),
            pltpu.VMEM((CLASS, TOK, columns), BF16),
            pltpu.VMEM((Z - 1, TOK, columns), BF16),
            pltpu.VMEM((ROWS, inputs.shape[0] // ROWS, depth), F32),
            pltpu.VMEM((ROWS - 1, inputs.shape[0] // ROWS, depth), F32),
            dma((len(WINDOW),)), dma((len(WINDOW),)), dma((len(FAR),)), dma((len(FAR),)),
            dma((len(FAR),)), dma((len(FAR),)), dma((6,)), dma((6,)), dma((21,)), dma((21,)),
            dma((pieces, Y - 1)), dma((pieces, Y - 1)), dma((pieces, 4)), dma((pieces, 4)),
            dma((pieces, Z - 1)), dma((pieces, Z - 1)),
            dma((ROWS - 1,)), dma((ROWS - 1,)),
        ],
        compiler_params=pltpu.CompilerParams(
            collective_id=0, has_side_effects=True, vmem_limit_bytes=56 * 2**20
        ),
        name="joined_projection",
    )(inputs, weight, out_grad)
    return pl.pallas_call(
        hand_over,
        out_shape=tuple(jax.ShapeDtypeStruct(a.shape, a.dtype) for a in results),
        in_specs=[anywhere] * 3,
        out_specs=(anywhere,) * 3,
        scratch_shapes=[pltpu.VMEM(a.shape, a.dtype) for a in results] + [dma((6,)), dma((6,))],
        name="hand_over",
    )(*results)


def solution(mesh):
    placed = (P(None, "ka"), P("row", "ka"), P("ka", "row"))
    return jax.shard_map(
        local,
        mesh=mesh,
        in_specs=placed,
        out_specs=(P("ka", "row"), P("row", "ka"), P("row", "ka")),
        check_vma=False,
    )
```

```python
import functools
import math

import jax
import jax.numpy as jnp
import numpy as np
from jax import lax
from jax.experimental import pallas as pl
from jax.experimental.pallas import tpu as pltpu
from jax.sharding import PartitionSpec as P

LEVELS = 7
MESH = pl.DeviceIdType.MESH
F32 = jnp.float32
BF16 = jnp.bfloat16

Z, Y, TOK = 16, 4, 4
CLASS = Z // 4
ROWS = 8
PIECES = (256, 512, 512, 512, 256, 256)
DIRECT = 4

WINDOW = [(dy, dz) for dz in (2, 1, -1, 0) for dy in range(Y) if (dy, dz) != (0, 0)]
FAR = (8, 4, 12)
NEAR = (2, 1, 15)
AROUND = (8, 7, 9, 6, 10, 5, 11, 4, 12, 3, 13, 2, 14, 1, 15)


def sine_terms():
    nodes = 0.5 * np.cos((np.arange(4000) + 0.5) * np.pi / 8000)
    t = nodes * nodes
    basis = np.stack([t**k for k in range(7)], axis=1)
    scale = nodes[:, None]
    terms, *_ = np.linalg.lstsq(basis * scale, np.sin(2 * np.pi * nodes), rcond=None)
    return [float(c) for c in terms]


def quantized_block(wide, inverse, share, terms):
    turns = wide * inverse
    rest = turns - jnp.round(turns)
    square = rest * rest
    value = terms[-1] * square + terms[-2]
    for term in terms[-3::-1]:
        value = value * square + term
    return (wide - share * (rest * value)).astype(BF16)


def kernel(
    x_hbm, w_hbm, g_hbm, projected_hbm, input_hbm, weight_hbm,
    projected_ref, input_ref, weight_ref, store_sem, x_ref, w_ref, g_ref, load_sem, wt, qt, gathered, x_by_y, x_by_class, peak_own, peak_near, peak_mid, peak_far,
    part, part_in, sums, near_in, sums_far, sums_in, grad, grad_in,
    near_s, near_r, far_s, far_r, g1_s, g1_r, g2_s, g2_r, g3_s, g3_r,
    part_s, part_r, part_near_s, part_near_r, sums_s, sums_r, grad_s, grad_r,
):
    ka, row = lax.axis_index("ka"), lax.axis_index("row")
    z, y = ka // Y, ka % Y
    low, high = z % 4, z // 4
    columns = w_hbm.shape[0]
    terms = sine_terms()

    def at(dz, dy):
        return (lax.rem(z + dz + Z, Z) * Y + lax.rem(y + dy, Y), row)

    def beside(d):
        return (ka, lax.rem(row + d, ROWS))

    def send(source, target, sent, arrived, device):
        copy = pltpu.make_async_remote_copy(
            src_ref=source, dst_ref=target, send_sem=sent, recv_sem=arrived,
            device_id=device, device_id_type=MESH,
        )
        copy.start()
        return copy

    barrier = pltpu.get_barrier_semaphore()
    greeted = [at(dz, 0) for dz in AROUND if dz not in (1, 2, 15)]
    greeted += [at(-dz, dy) for dy, dz in WINDOW] + [beside(d) for d in range(1, ROWS)]
    for device in greeted:
        pl.semaphore_signal(barrier, inc=1, device_id=device, device_id_type=MESH)

    loads = [
        pltpu.make_async_copy(source, target, load_sem.at[i])
        for i, (source, target) in enumerate(((w_hbm, w_ref), (g_hbm, g_ref), (x_hbm, x_ref)))
    ]
    for copy in loads:
        copy.start()

    loads[0].wait()
    for c in range(0, columns, 256):
        wt[:, c : c + 256] = w_ref[c : c + 256, :].T
    peak = jnp.max(jnp.abs(wt[...].astype(F32)), axis=0, keepdims=True)
    peak = jnp.concatenate([peak[:, : columns // 2], peak[:, columns // 2 :]], axis=0)
    peak_own[...] = peak.astype(BF16)
    slot = low * 16 + y * CLASS + high
    loads[1].wait()
    loads[2].wait()
    gathered[slot] = g_ref[...]

    pl.semaphore_wait(barrier, len(greeted))

    near = [
        send(peak_own, peak_near.at[i], near_s.at[i], near_r.at[i], at(dz, dy))
        for i, (dy, dz) in enumerate(WINDOW)
    ]
    gather1 = [
        send(gathered.at[slot], gathered.at[slot], g1_s.at[i], g1_r.at[i], at(dz, 0))
        for i, dz in enumerate(FAR)
    ]

    to = lax.broadcasted_iota(jnp.int32, (256, 256), 0)
    come = lax.broadcasted_iota(jnp.int32, (256, 256), 1)
    by_y = to % 64 // TOK * 16 + to // 64 * TOK + to % TOK
    by_class = to // 64 * 16 + to // 16 % 4 * TOK + to // 4 % 4 * 64 + to % TOK
    for source, target in ((by_y, x_by_y), (by_class, x_by_class)):
        order = jnp.where(come == source, 1.0, 0.0).astype(BF16)
        target[...] = jnp.dot(order, x_ref[...], preferred_element_type=F32).astype(BF16)

    for i, copy in enumerate(near):
        copy.wait_recv()
        peak = jnp.maximum(peak, peak_near[i].astype(F32))
    peak_mid[...] = peak.astype(BF16)
    far = [
        send(peak_mid, peak_far.at[i], far_s.at[i], far_r.at[i], at(dz, 0))
        for i, dz in enumerate(FAR)
    ]

    for copy in gather1:
        copy.wait_recv()
    held = gathered.at[pl.ds(low * 16 + y * CLASS, CLASS)]
    gather2 = [
        send(held, held, g2_s.at[i], g2_r.at[i], device)
        for i, device in enumerate([at(dz, 0) for dz in NEAR] + [at(0, dy) for dy in (2, 1, 3)])
    ]

    for i, copy in enumerate(far):
        copy.wait_recv()
        peak = jnp.maximum(peak, peak_far[i].astype(F32))
    peak = jnp.concatenate([peak[0:1], peak[1:2]], axis=1)
    inverse = LEVELS / peak
    share = peak * (1.0 / (LEVELS * 2.0 * math.pi))

    starts = [sum(PIECES[:p]) for p in range(len(PIECES))]
    spans = [slice(s, s + n) for s, n in zip(starts, PIECES)]
    by_y, gather3 = [], []
    for p, span in enumerate(spans):
        for c in range(span.start, span.stop, 256):
            block = slice(c, c + 256)
            qt[:, block] = quantized_block(
                wt[:, block].astype(F32), inverse[:, block], share[:, block], terms
            )
            product = jnp.dot(x_by_y[...], qt[:, block], preferred_element_type=F32)
            part[:, :, block] = product.astype(BF16).reshape(Y, 64, 256)
        cut = pl.ds(span.start, PIECES[p])
        by_y.append([
            send(
                part.at[lax.rem(y + dy, Y), :, cut], part_in.at[i, :, cut],
                part_s.at[p, i], part_r.at[p, i], at(0, dy),
            )
            for i, dy in enumerate((2, 1, 3))
        ])
        if p == 0:
            for copy in gather2:
                copy.wait_recv()
            for dy in (2, 1, 3):
                held_y = low * 16 + lax.rem(y + dy, Y) * CLASS
                for dz, start, size in ((1, 0, 3), (15, 0, 3), (2, 0, 2), (14, 2, 1)):
                    i = len(gather3)
                    held = gathered.at[pl.ds(held_y + start, size)]
                    gather3.append(send(held, held, g3_s.at[i], g3_r.at[i], at(dz, 0)))
        if p == 3:
            for dz in (1, 2, 3):
                held = gathered.at[pl.ds(lax.rem(low + dz, 4) * 16 + y * CLASS + 3, 1)]
                for dy in (2, 1, 3):
                    i = len(gather3)
                    gather3.append(send(held, held, g3_s.at[i], g3_r.at[i], at(0, dy)))

    def chunk(k):
        return lax.rem(k, 4) * CLASS + k // 4

    def near_total(p):
        span, cut = spans[p], pl.ds(spans[p].start, PIECES[p])
        for copy in by_near[p]:
            copy.wait_recv()
        total = sums[pl.ds(low * CLASS, CLASS), :, span].astype(F32)
        for i in range(3):
            total += near_in[i, :, :, span].astype(F32)
        sums_far[:, :, span] = total.astype(BF16)
        by_z[p] = [
            send(
                sums_far.at[lax.rem(high + m, CLASS), :, cut], sums_in.at[i, :, cut],
                sums_s.at[p, i], sums_r.at[p, i], at(4 * m, 0),
            )
            for i, m in enumerate((2, 1, 3))
        ]

    by_z, by_near = {}, {}
    for p, span in enumerate(spans):
        for copy in by_y[p]:
            copy.wait_recv()
        total = part[y, :, span].astype(F32)
        for i in range(3):
            total += part_in[i, :, span].astype(F32)
        for k in range(Z):
            sums[k % 4 * CLASS + k // 4, :, span] = total[TOK * k : TOK * k + TOK, :].astype(BF16)
        cut = pl.ds(span.start, PIECES[p])
        if p >= len(PIECES) - DIRECT:
            by_z[p] = [
                send(
                    sums.at[chunk(lax.rem(z + dz, Z)), :, cut], sums_in.at[i, :, cut],
                    sums_s.at[p, i], sums_r.at[p, i], at(dz, 0),
                )
                for i, dz in enumerate(AROUND)
            ]
        else:
            by_near[p] = [
                send(
                    sums.at[pl.ds(lax.rem(low + dz, 4) * CLASS + first, count), :, cut],
                    near_in.at[i, pl.ds(first, count), :, cut],
                    part_near_s.at[p, j], part_near_r.at[p, j], at(dz, 0),
                )
                for j, (i, dz, first, count) in enumerate(
                    ((0, 1, 0, 4), (1, 15, 0, 4), (2, 2, 0, 2), (2, 14, 2, 2))
                )
            ]
        if p >= 1 and p - 1 in by_near:
            near_total(p - 1)
    if not DIRECT:
        near_total(len(PIECES) - 1)

    for copy in gather3:
        copy.wait_recv()
    tokens = gathered[...].reshape(256, columns)
    product = lax.dot_general(
        tokens, qt[...], (((1,), (1,)), ((), ())), preferred_element_type=F32
    )
    for k in range(Y * Z):
        start = k // Y % 4 * 64 + k % Y * 16 + k // 16 * TOK
        grad[k // 8, k % 8 * TOK : k % 8 * TOK + TOK, :] = product[start : start + TOK, :]
    by_row = [
        send(
            grad.at[lax.rem(row + d, ROWS)], grad_in.at[d - 1],
            grad_s.at[d - 1], grad_r.at[d - 1], beside(d),
        )
        for d in range(1, ROWS)
    ]

    for c in range(0, columns, 256):
        block = gathered[:, :, c : c + 256].reshape(256, 256)
        product = lax.dot_general(
            block, x_by_class[...], (((0,), (0,)), ((), ())), preferred_element_type=F32
        )
        weight_ref[c : c + 256, :] = (product * (1.0 / math.sqrt(x_hbm.shape[0]))).astype(BF16)

    stores = [
        pltpu.make_async_copy(source, target, store_sem.at[i])
        for i, (source, target) in enumerate(
            ((weight_ref, weight_hbm), (input_ref, input_hbm), (projected_ref, projected_hbm))
        )
    ]
    stores[0].start()

    total = grad[row]
    for i, copy in enumerate(by_row):
        copy.wait_recv()
        total += grad_in[i]
    input_ref[...] = total.astype(BF16)
    stores[1].start()

    for p, span in enumerate(spans):
        direct = p >= len(PIECES) - DIRECT
        total = (sums[chunk(z), :, span] if direct else sums_far[high, :, span]).astype(F32)
        for i, copy in enumerate(by_z[p]):
            copy.wait_recv()
            total += sums_in[i, :, span].astype(F32)
        projected_ref[:, span] = total.astype(BF16)
    stores[2].start()

    for copy in near + far + gather1 + gather2 + gather3 + by_row + sum(by_y, []):
        copy.wait_send()
    for copy in sum(by_near.values(), []) + sum(by_z.values(), []):
        copy.wait_send()
    for copy in stores:
        copy.wait()


def hand_over(*refs):
    sources, targets, held, came, done = refs[:3], refs[3:6], refs[6:9], refs[9], refs[10]
    moves = []
    for source, target, here in zip(sources, targets, held):
        rows = source.shape[0]
        parts = 4 if rows >= 2048 else 1
        for k in range(parts):
            cut, i = pl.ds(k * (rows // parts), rows // parts), len(moves)
            moves.append((
                pltpu.make_async_copy(source.at[cut], here.at[cut], came.at[i]),
                pltpu.make_async_copy(here.at[cut], target.at[cut], done.at[i]),
            ))
    for come, _ in moves:
        come.start()
    for come, go in moves:
        come.wait()
        go.start()
    for _, go in moves:
        go.wait()


def local(inputs, weight, out_grad):
    columns, depth = weight.shape
    pieces = len(PIECES)
    anywhere = pl.BlockSpec(memory_space=pl.ANY)
    dma = pltpu.SemaphoreType.DMA
    results = pl.pallas_call(
        kernel,
        out_shape=(
            jax.ShapeDtypeStruct(out_grad.shape, BF16),
            jax.ShapeDtypeStruct((inputs.shape[0] // ROWS, depth), BF16),
            jax.ShapeDtypeStruct(weight.shape, BF16),
        ),
        in_specs=[anywhere] * 3,
        out_specs=(anywhere,) * 3,
        scratch_shapes=[
            pltpu.VMEM(out_grad.shape, BF16),
            pltpu.VMEM((inputs.shape[0] // ROWS, depth), BF16),
            pltpu.VMEM(weight.shape, BF16),
            dma((3,)),
            pltpu.VMEM(inputs.shape, BF16),
            pltpu.VMEM(weight.shape, BF16),
            pltpu.VMEM(out_grad.shape, BF16),
            dma((3,)),
            pltpu.VMEM((depth, columns), BF16),
            pltpu.VMEM((depth, columns), BF16),
            pltpu.VMEM((Y * Z, TOK, columns), BF16),
            pltpu.VMEM(inputs.shape, BF16),
            pltpu.VMEM(inputs.shape, BF16),
            pltpu.VMEM((2, columns // 2), BF16),
            pltpu.VMEM((len(WINDOW), 2, columns // 2), BF16),
            pltpu.VMEM((2, columns // 2), BF16),
            pltpu.VMEM((len(FAR), 2, columns // 2), BF16),
            pltpu.VMEM((Y, Z * TOK, columns), BF16),
            pltpu.VMEM((Y - 1, Z * TOK, columns), BF16),
            pltpu.VMEM((Z, TOK, columns), BF16),
            pltpu.VMEM((3, CLASS, TOK, columns), BF16),
            pltpu.VMEM((CLASS, TOK, columns), BF16),
            pltpu.VMEM((Z - 1, TOK, columns), BF16),
            pltpu.VMEM((ROWS, inputs.shape[0] // ROWS, depth), F32),
            pltpu.VMEM((ROWS - 1, inputs.shape[0] // ROWS, depth), F32),
            dma((len(WINDOW),)), dma((len(WINDOW),)), dma((len(FAR),)), dma((len(FAR),)),
            dma((len(FAR),)), dma((len(FAR),)), dma((6,)), dma((6,)), dma((21,)), dma((21,)),
            dma((pieces, Y - 1)), dma((pieces, Y - 1)), dma((pieces, 4)), dma((pieces, 4)),
            dma((pieces, Z - 1)), dma((pieces, Z - 1)),
            dma((ROWS - 1,)), dma((ROWS - 1,)),
        ],
        compiler_params=pltpu.CompilerParams(
            collective_id=0, has_side_effects=True, vmem_limit_bytes=56 * 2**20
        ),
        name="joined_projection",
    )(inputs, weight, out_grad)
    return pl.pallas_call(
        hand_over,
        out_shape=tuple(jax.ShapeDtypeStruct(a.shape, a.dtype) for a in results),
        in_specs=[anywhere] * 3,
        out_specs=(anywhere,) * 3,
        scratch_shapes=[pltpu.VMEM(a.shape, a.dtype) for a in results] + [dma((6,)), dma((6,))],
        name="hand_over",
    )(*results)


def solution(mesh):
    placed = (P(None, "ka"), P("row", "ka"), P("ka", "row"))
    return jax.shard_map(
        local,
        mesh=mesh,
        in_specs=placed,
        out_specs=(P("ka", "row"), P("row", "ka"), P("row", "ka")),
        check_vma=False,
    )
```

```python
import functools
import math

import jax
import jax.numpy as jnp
import numpy as np
from jax import lax
from jax.experimental import pallas as pl
from jax.experimental.pallas import tpu as pltpu
from jax.sharding import PartitionSpec as P

LEVELS = 7
MESH = pl.DeviceIdType.MESH
F32 = jnp.float32
BF16 = jnp.bfloat16

Z, Y, TOK = 16, 4, 4
CLASS = Z // 4
ROWS = 8
PIECES = (512, 512, 512, 256, 256, 256)
DIRECT = 4

WINDOW = [(dy, dz) for dz in (2, 1, -1, 0) for dy in range(Y) if (dy, dz) != (0, 0)]
FAR = (8, 4, 12)
NEAR = (2, 1, 15)
AROUND = (8, 7, 9, 6, 10, 5, 11, 4, 12, 3, 13, 2, 14, 1, 15)


def sine_terms():
    nodes = 0.5 * np.cos((np.arange(4000) + 0.5) * np.pi / 8000)
    t = nodes * nodes
    basis = np.stack([t**k for k in range(7)], axis=1)
    scale = nodes[:, None]
    terms, *_ = np.linalg.lstsq(basis * scale, np.sin(2 * np.pi * nodes), rcond=None)
    return [float(c) for c in terms]


def quantized_block(wide, inverse, share, terms):
    turns = wide * inverse
    rest = turns - jnp.round(turns)
    square = rest * rest
    value = terms[-1] * square + terms[-2]
    for term in terms[-3::-1]:
        value = value * square + term
    return (wide - share * (rest * value)).astype(BF16)


def kernel(
    x_hbm, w_hbm, g_hbm, projected_hbm, input_hbm, weight_hbm,
    projected_ref, input_ref, weight_ref, store_sem, x_ref, w_ref, g_ref, load_sem, wt, qt, gathered, x_by_y, x_by_class, peak_own, peak_near, peak_mid, peak_far,
    part, part_in, sums, near_in, sums_far, sums_in, grad, grad_in,
    near_s, near_r, far_s, far_r, g1_s, g1_r, g2_s, g2_r, g3_s, g3_r,
    part_s, part_r, part_near_s, part_near_r, sums_s, sums_r, grad_s, grad_r,
):
    ka, row = lax.axis_index("ka"), lax.axis_index("row")
    z, y = ka // Y, ka % Y
    low, high = z % 4, z // 4
    columns = w_hbm.shape[0]
    terms = sine_terms()

    def at(dz, dy):
        return (lax.rem(z + dz + Z, Z) * Y + lax.rem(y + dy, Y), row)

    def beside(d):
        return (ka, lax.rem(row + d, ROWS))

    def send(source, target, sent, arrived, device):
        copy = pltpu.make_async_remote_copy(
            src_ref=source, dst_ref=target, send_sem=sent, recv_sem=arrived,
            device_id=device, device_id_type=MESH,
        )
        copy.start()
        return copy

    barrier = pltpu.get_barrier_semaphore()
    greeted = [at(dz, 0) for dz in AROUND if dz not in (1, 2, 15)]
    greeted += [at(-dz, dy) for dy, dz in WINDOW] + [beside(d) for d in range(1, ROWS)]
    for device in greeted:
        pl.semaphore_signal(barrier, inc=1, device_id=device, device_id_type=MESH)

    loads = [
        pltpu.make_async_copy(source, target, load_sem.at[i])
        for i, (source, target) in enumerate(((w_hbm, w_ref), (g_hbm, g_ref), (x_hbm, x_ref)))
    ]
    for copy in loads:
        copy.start()

    loads[0].wait()
    for c in range(0, columns, 256):
        wt[:, c : c + 256] = w_ref[c : c + 256, :].T
    peak = jnp.max(jnp.abs(wt[...].astype(F32)), axis=0, keepdims=True)
    peak = jnp.concatenate([peak[:, : columns // 2], peak[:, columns // 2 :]], axis=0)
    peak_own[...] = peak.astype(BF16)
    slot = low * 16 + y * CLASS + high
    loads[1].wait()
    loads[2].wait()
    gathered[slot] = g_ref[...]

    pl.semaphore_wait(barrier, len(greeted))

    near = [
        send(peak_own, peak_near.at[i], near_s.at[i], near_r.at[i], at(dz, dy))
        for i, (dy, dz) in enumerate(WINDOW)
    ]
    gather1 = [
        send(gathered.at[slot], gathered.at[slot], g1_s.at[i], g1_r.at[i], at(dz, 0))
        for i, dz in enumerate(FAR)
    ]

    to = lax.broadcasted_iota(jnp.int32, (256, 256), 0)
    come = lax.broadcasted_iota(jnp.int32, (256, 256), 1)
    by_y = to % 64 // TOK * 16 + to // 64 * TOK + to % TOK
    by_class = to // 64 * 16 + to // 16 % 4 * TOK + to // 4 % 4 * 64 + to % TOK
    for source, target in ((by_y, x_by_y), (by_class, x_by_class)):
        order = jnp.where(come == source, 1.0, 0.0).astype(BF16)
        target[...] = jnp.dot(order, x_ref[...], preferred_element_type=F32).astype(BF16)

    for i, copy in enumerate(near):
        copy.wait_recv()
        peak = jnp.maximum(peak, peak_near[i].astype(F32))
    peak_mid[...] = peak.astype(BF16)
    far = [
        send(peak_mid, peak_far.at[i], far_s.at[i], far_r.at[i], at(dz, 0))
        for i, dz in enumerate(FAR)
    ]

    for copy in gather1:
        copy.wait_recv()
    held = gathered.at[pl.ds(low * 16 + y * CLASS, CLASS)]
    gather2 = [
        send(held, held, g2_s.at[i], g2_r.at[i], device)
        for i, device in enumerate([at(dz, 0) for dz in NEAR] + [at(0, dy) for dy in (2, 1, 3)])
    ]

    for i, copy in enumerate(far):
        copy.wait_recv()
        peak = jnp.maximum(peak, peak_far[i].astype(F32))
    peak = jnp.concatenate([peak[0:1], peak[1:2]], axis=1)
    inverse = LEVELS / peak
    share = peak * (1.0 / (LEVELS * 2.0 * math.pi))

    starts = [sum(PIECES[:p]) for p in range(len(PIECES))]
    spans = [slice(s, s + n) for s, n in zip(starts, PIECES)]
    by_y, gather3 = [], []
    for p, span in enumerate(spans):
        for c in range(span.start, span.stop, 256):
            block = slice(c, c + 256)
            qt[:, block] = quantized_block(
                wt[:, block].astype(F32), inverse[:, block], share[:, block], terms
            )
            product = jnp.dot(x_by_y[...], qt[:, block], preferred_element_type=F32)
            part[:, :, block] = product.astype(BF16).reshape(Y, 64, 256)
        cut = pl.ds(span.start, PIECES[p])
        by_y.append([
            send(
                part.at[lax.rem(y + dy, Y), :, cut], part_in.at[i, :, cut],
                part_s.at[p, i], part_r.at[p, i], at(0, dy),
            )
            for i, dy in enumerate((2, 1, 3))
        ])
        if p == 0:
            for copy in gather2:
                copy.wait_recv()
            for dy in (2, 1, 3):
                held_y = low * 16 + lax.rem(y + dy, Y) * CLASS
                for dz, start, size in ((1, 0, 3), (15, 0, 3), (2, 0, 2), (14, 2, 1)):
                    i = len(gather3)
                    held = gathered.at[pl.ds(held_y + start, size)]
                    gather3.append(send(held, held, g3_s.at[i], g3_r.at[i], at(dz, 0)))
        if p == 3:
            for dz in (1, 2, 3):
                held = gathered.at[pl.ds(lax.rem(low + dz, 4) * 16 + y * CLASS + 3, 1)]
                for dy in (2, 1, 3):
                    i = len(gather3)
                    gather3.append(send(held, held, g3_s.at[i], g3_r.at[i], at(0, dy)))

    def chunk(k):
        return lax.rem(k, 4) * CLASS + k // 4

    def near_total(p):
        span, cut = spans[p], pl.ds(spans[p].start, PIECES[p])
        for copy in by_near[p]:
            copy.wait_recv()
        total = sums[pl.ds(low * CLASS, CLASS), :, span].astype(F32)
        for i in range(3):
            total += near_in[i, :, :, span].astype(F32)
        sums_far[:, :, span] = total.astype(BF16)
        by_z[p] = [
            send(
                sums_far.at[lax.rem(high + m, CLASS), :, cut], sums_in.at[i, :, cut],
                sums_s.at[p, i], sums_r.at[p, i], at(4 * m, 0),
            )
            for i, m in enumerate((2, 1, 3))
        ]

    by_z, by_near = {}, {}
    for p, span in enumerate(spans):
        for copy in by_y[p]:
            copy.wait_recv()
        total = part[y, :, span].astype(F32)
        for i in range(3):
            total += part_in[i, :, span].astype(F32)
        for k in range(Z):
            sums[k % 4 * CLASS + k // 4, :, span] = total[TOK * k : TOK * k + TOK, :].astype(BF16)
        cut = pl.ds(span.start, PIECES[p])
        if p >= len(PIECES) - DIRECT:
            by_z[p] = [
                send(
                    sums.at[chunk(lax.rem(z + dz, Z)), :, cut], sums_in.at[i, :, cut],
                    sums_s.at[p, i], sums_r.at[p, i], at(dz, 0),
                )
                for i, dz in enumerate(AROUND)
            ]
        else:
            by_near[p] = [
                send(
                    sums.at[pl.ds(lax.rem(low + dz, 4) * CLASS + first, count), :, cut],
                    near_in.at[i, pl.ds(first, count), :, cut],
                    part_near_s.at[p, j], part_near_r.at[p, j], at(dz, 0),
                )
                for j, (i, dz, first, count) in enumerate(
                    ((0, 1, 0, 4), (1, 15, 0, 4), (2, 2, 0, 2), (2, 14, 2, 2))
                )
            ]
        if p >= 1 and p - 1 in by_near:
            near_total(p - 1)
    if not DIRECT:
        near_total(len(PIECES) - 1)

    for copy in gather3:
        copy.wait_recv()
    tokens = gathered[...].reshape(256, columns)
    product = lax.dot_general(
        tokens, qt[...], (((1,), (1,)), ((), ())), preferred_element_type=F32
    )
    for k in range(Y * Z):
        start = k // Y % 4 * 64 + k % Y * 16 + k // 16 * TOK
        grad[k // 8, k % 8 * TOK : k % 8 * TOK + TOK, :] = product[start : start + TOK, :]
    by_row = [
        send(
            grad.at[lax.rem(row + d, ROWS)], grad_in.at[d - 1],
            grad_s.at[d - 1], grad_r.at[d - 1], beside(d),
        )
        for d in range(1, ROWS)
    ]

    for c in range(0, columns, 256):
        block = gathered[:, :, c : c + 256].reshape(256, 256)
        product = lax.dot_general(
            block, x_by_class[...], (((0,), (0,)), ((), ())), preferred_element_type=F32
        )
        weight_ref[c : c + 256, :] = (product * (1.0 / math.sqrt(x_hbm.shape[0]))).astype(BF16)

    stores = [
        pltpu.make_async_copy(source, target, store_sem.at[i])
        for i, (source, target) in enumerate(
            ((weight_ref, weight_hbm), (input_ref, input_hbm), (projected_ref, projected_hbm))
        )
    ]
    stores[0].start()

    total = grad[row]
    for i, copy in enumerate(by_row):
        copy.wait_recv()
        total += grad_in[i]
    input_ref[...] = total.astype(BF16)
    stores[1].start()

    for p, span in enumerate(spans):
        direct = p >= len(PIECES) - DIRECT
        total = (sums[chunk(z), :, span] if direct else sums_far[high, :, span]).astype(F32)
        for i, copy in enumerate(by_z[p]):
            copy.wait_recv()
            total += sums_in[i, :, span].astype(F32)
        projected_ref[:, span] = total.astype(BF16)
    stores[2].start()

    for copy in near + far + gather1 + gather2 + gather3 + by_row + sum(by_y, []):
        copy.wait_send()
    for copy in sum(by_near.values(), []) + sum(by_z.values(), []):
        copy.wait_send()
    for copy in stores:
        copy.wait()


def hand_over(*refs):
    sources, targets, held, came, done = refs[:3], refs[3:6], refs[6:9], refs[9], refs[10]
    moves = []
    for source, target, here in zip(sources, targets, held):
        rows = source.shape[0]
        parts = 4 if rows >= 2048 else 1
        for k in range(parts):
            cut, i = pl.ds(k * (rows // parts), rows // parts), len(moves)
            moves.append((
                pltpu.make_async_copy(source.at[cut], here.at[cut], came.at[i]),
                pltpu.make_async_copy(here.at[cut], target.at[cut], done.at[i]),
            ))
    for come, _ in moves:
        come.start()
    for come, go in moves:
        come.wait()
        go.start()
    for _, go in moves:
        go.wait()


def local(inputs, weight, out_grad):
    columns, depth = weight.shape
    pieces = len(PIECES)
    anywhere = pl.BlockSpec(memory_space=pl.ANY)
    dma = pltpu.SemaphoreType.DMA
    results = pl.pallas_call(
        kernel,
        out_shape=(
            jax.ShapeDtypeStruct(out_grad.shape, BF16),
            jax.ShapeDtypeStruct((inputs.shape[0] // ROWS, depth), BF16),
            jax.ShapeDtypeStruct(weight.shape, BF16),
        ),
        in_specs=[anywhere] * 3,
        out_specs=(anywhere,) * 3,
        scratch_shapes=[
            pltpu.VMEM(out_grad.shape, BF16),
            pltpu.VMEM((inputs.shape[0] // ROWS, depth), BF16),
            pltpu.VMEM(weight.shape, BF16),
            dma((3,)),
            pltpu.VMEM(inputs.shape, BF16),
            pltpu.VMEM(weight.shape, BF16),
            pltpu.VMEM(out_grad.shape, BF16),
            dma((3,)),
            pltpu.VMEM((depth, columns), BF16),
            pltpu.VMEM((depth, columns), BF16),
            pltpu.VMEM((Y * Z, TOK, columns), BF16),
            pltpu.VMEM(inputs.shape, BF16),
            pltpu.VMEM(inputs.shape, BF16),
            pltpu.VMEM((2, columns // 2), BF16),
            pltpu.VMEM((len(WINDOW), 2, columns // 2), BF16),
            pltpu.VMEM((2, columns // 2), BF16),
            pltpu.VMEM((len(FAR), 2, columns // 2), BF16),
            pltpu.VMEM((Y, Z * TOK, columns), BF16),
            pltpu.VMEM((Y - 1, Z * TOK, columns), BF16),
            pltpu.VMEM((Z, TOK, columns), BF16),
            pltpu.VMEM((3, CLASS, TOK, columns), BF16),
            pltpu.VMEM((CLASS, TOK, columns), BF16),
            pltpu.VMEM((Z - 1, TOK, columns), BF16),
            pltpu.VMEM((ROWS, inputs.shape[0] // ROWS, depth), F32),
            pltpu.VMEM((ROWS - 1, inputs.shape[0] // ROWS, depth), F32),
            dma((len(WINDOW),)), dma((len(WINDOW),)), dma((len(FAR),)), dma((len(FAR),)),
            dma((len(FAR),)), dma((len(FAR),)), dma((6,)), dma((6,)), dma((21,)), dma((21,)),
            dma((pieces, Y - 1)), dma((pieces, Y - 1)), dma((pieces, 4)), dma((pieces, 4)),
            dma((pieces, Z - 1)), dma((pieces, Z - 1)),
            dma((ROWS - 1,)), dma((ROWS - 1,)),
        ],
        compiler_params=pltpu.CompilerParams(
            collective_id=0, has_side_effects=True, vmem_limit_bytes=56 * 2**20
        ),
        name="joined_projection",
    )(inputs, weight, out_grad)
    return pl.pallas_call(
        hand_over,
        out_shape=tuple(jax.ShapeDtypeStruct(a.shape, a.dtype) for a in results),
        in_specs=[anywhere] * 3,
        out_specs=(anywhere,) * 3,
        scratch_shapes=[pltpu.VMEM(a.shape, a.dtype) for a in results] + [dma((6,)), dma((6,))],
        name="hand_over",
    )(*results)


def solution(mesh):
    placed = (P(None, "ka"), P("row", "ka"), P("ka", "row"))
    return jax.shard_map(
        local,
        mesh=mesh,
        in_specs=placed,
        out_specs=(P("ka", "row"), P("row", "ka"), P("row", "ka")),
        check_vma=False,
    )
```

```python
import functools
import math

import jax
import jax.numpy as jnp
import numpy as np
from jax import lax
from jax.experimental import pallas as pl
from jax.experimental.pallas import tpu as pltpu
from jax.sharding import PartitionSpec as P

LEVELS = 7
MESH = pl.DeviceIdType.MESH
F32 = jnp.float32
BF16 = jnp.bfloat16

Z, Y, TOK = 16, 4, 4
CLASS = Z // 4
ROWS = 8
PIECES = (512, 512, 512, 256, 256, 256)
DIRECT = 4

WINDOW = [(dy, dz) for dz in (2, 1, -1, 0) for dy in range(Y) if (dy, dz) != (0, 0)]
FAR = (8, 4, 12)
NEAR = (2, 1, 15)
AROUND = (8, 7, 9, 6, 10, 5, 11, 4, 12, 3, 13, 2, 14, 1, 15)


def sine_terms():
    nodes = 0.5 * np.cos((np.arange(4000) + 0.5) * np.pi / 8000)
    t = nodes * nodes
    basis = np.stack([t**k for k in range(7)], axis=1)
    scale = nodes[:, None]
    terms, *_ = np.linalg.lstsq(basis * scale, np.sin(2 * np.pi * nodes), rcond=None)
    return [float(c) for c in terms]


def quantized_block(wide, inverse, share, terms):
    turns = wide * inverse
    rest = turns - jnp.round(turns)
    square = rest * rest
    value = terms[-1] * square + terms[-2]
    for term in terms[-3::-1]:
        value = value * square + term
    return (wide - share * (rest * value)).astype(BF16)


def kernel(
    x_hbm, w_hbm, g_hbm, projected_hbm, input_hbm, weight_hbm,
    projected_ref, input_ref, weight_ref, store_sem, x_ref, w_ref, g_ref, load_sem, wt, qt, gathered, x_by_y, x_by_class, peak_own, peak_near, peak_mid, peak_far,
    part, part_in, sums, near_in, sums_far, sums_in, grad, grad_in,
    near_s, near_r, far_s, far_r, g1_s, g1_r, g2_s, g2_r, g3_s, g3_r,
    part_s, part_r, part_near_s, part_near_r, sums_s, sums_r, grad_s, grad_r,
):
    ka, row = lax.axis_index("ka"), lax.axis_index("row")
    z, y = ka // Y, ka % Y
    low, high = z % 4, z // 4
    columns = w_hbm.shape[0]
    terms = sine_terms()

    def at(dz, dy):
        return (lax.rem(z + dz + Z, Z) * Y + lax.rem(y + dy, Y), row)

    def beside(d):
        return (ka, lax.rem(row + d, ROWS))

    def send(source, target, sent, arrived, device):
        copy = pltpu.make_async_remote_copy(
            src_ref=source, dst_ref=target, send_sem=sent, recv_sem=arrived,
            device_id=device, device_id_type=MESH,
        )
        copy.start()
        return copy

    barrier = pltpu.get_barrier_semaphore()
    greeted = [at(dz, 0) for dz in AROUND if dz not in (1, 2, 15)]
    greeted += [at(-dz, dy) for dy, dz in WINDOW] + [beside(d) for d in range(1, ROWS)]
    for device in greeted:
        pl.semaphore_signal(barrier, inc=1, device_id=device, device_id_type=MESH)

    loads = [
        pltpu.make_async_copy(source, target, load_sem.at[i])
        for i, (source, target) in enumerate(((w_hbm, w_ref), (g_hbm, g_ref), (x_hbm, x_ref)))
    ]
    for copy in loads:
        copy.start()

    loads[0].wait()
    for c in range(0, columns, 256):
        wt[:, c : c + 256] = w_ref[c : c + 256, :].T
    peak = jnp.max(jnp.abs(wt[...].astype(F32)), axis=0, keepdims=True)
    peak = jnp.concatenate([peak[:, : columns // 2], peak[:, columns // 2 :]], axis=0)
    peak_own[...] = peak.astype(BF16)
    slot = low * 16 + y * CLASS + high
    loads[1].wait()
    loads[2].wait()
    gathered[slot] = g_ref[...]

    pl.semaphore_wait(barrier, len(greeted))

    near = [
        send(peak_own, peak_near.at[i], near_s.at[i], near_r.at[i], at(dz, dy))
        for i, (dy, dz) in enumerate(WINDOW)
    ]
    gather1 = [
        send(gathered.at[slot], gathered.at[slot], g1_s.at[i], g1_r.at[i], at(dz, 0))
        for i, dz in enumerate(FAR)
    ]

    to = lax.broadcasted_iota(jnp.int32, (256, 256), 0)
    come = lax.broadcasted_iota(jnp.int32, (256, 256), 1)
    by_y = to % 64 // TOK * 16 + to // 64 * TOK + to % TOK
    by_class = to // 64 * 16 + to // 16 % 4 * TOK + to // 4 % 4 * 64 + to % TOK
    for source, target in ((by_y, x_by_y), (by_class, x_by_class)):
        order = jnp.where(come == source, 1.0, 0.0).astype(BF16)
        target[...] = jnp.dot(order, x_ref[...], preferred_element_type=F32).astype(BF16)

    for i, copy in enumerate(near):
        copy.wait_recv()
        peak = jnp.maximum(peak, peak_near[i].astype(F32))
    peak_mid[...] = peak.astype(BF16)
    far = [
        send(peak_mid, peak_far.at[i], far_s.at[i], far_r.at[i], at(dz, 0))
        for i, dz in enumerate(FAR)
    ]

    for copy in gather1:
        copy.wait_recv()
    held = gathered.at[pl.ds(low * 16 + y * CLASS, CLASS)]
    gather2 = [
        send(held, held, g2_s.at[i], g2_r.at[i], device)
        for i, device in enumerate([at(dz, 0) for dz in NEAR] + [at(0, dy) for dy in (2, 1, 3)])
    ]

    for i, copy in enumerate(far):
        copy.wait_recv()
        peak = jnp.maximum(peak, peak_far[i].astype(F32))
    peak = jnp.concatenate([peak[0:1], peak[1:2]], axis=1)
    inverse = LEVELS / peak
    share = peak * (1.0 / (LEVELS * 2.0 * math.pi))

    starts = [sum(PIECES[:p]) for p in range(len(PIECES))]
    spans = [slice(s, s + n) for s, n in zip(starts, PIECES)]
    by_y, gather3 = [], []
    for p, span in enumerate(spans):
        for c in range(span.start, span.stop, 256):
            block = slice(c, c + 256)
            qt[:, block] = quantized_block(
                wt[:, block].astype(F32), inverse[:, block], share[:, block], terms
            )
            product = jnp.dot(x_by_y[...], qt[:, block], preferred_element_type=F32)
            part[:, :, block] = product.astype(BF16).reshape(Y, 64, 256)
        cut = pl.ds(span.start, PIECES[p])
        by_y.append([
            send(
                part.at[lax.rem(y + dy, Y), :, cut], part_in.at[i, :, cut],
                part_s.at[p, i], part_r.at[p, i], at(0, dy),
            )
            for i, dy in enumerate((2, 1, 3))
        ])
        if p == 0:
            for copy in gather2:
                copy.wait_recv()
            for dy in (2, 1, 3):
                held_y = low * 16 + lax.rem(y + dy, Y) * CLASS
                for dz, start, size in ((1, 0, 3), (15, 0, 3), (2, 0, 2), (14, 2, 1)):
                    i = len(gather3)
                    held = gathered.at[pl.ds(held_y + start, size)]
                    gather3.append(send(held, held, g3_s.at[i], g3_r.at[i], at(dz, 0)))
        if p == 3:
            for dz in (1, 2, 3):
                held = gathered.at[pl.ds(lax.rem(low + dz, 4) * 16 + y * CLASS + 3, 1)]
                for dy in (2, 1, 3):
                    i = len(gather3)
                    gather3.append(send(held, held, g3_s.at[i], g3_r.at[i], at(0, dy)))

    def chunk(k):
        return lax.rem(k, 4) * CLASS + k // 4

    def near_total(p):
        span, cut = spans[p], pl.ds(spans[p].start, PIECES[p])
        for copy in by_near[p]:
            copy.wait_recv()
        total = sums[pl.ds(low * CLASS, CLASS), :, span].astype(F32)
        for i in range(3):
            total += near_in[i, :, :, span].astype(F32)
        sums_far[:, :, span] = total.astype(BF16)
        by_z[p] = [
            send(
                sums_far.at[lax.rem(high + m, CLASS), :, cut], sums_in.at[i, :, cut],
                sums_s.at[p, i], sums_r.at[p, i], at(4 * m, 0),
            )
            for i, m in enumerate((2, 1, 3))
        ]

    by_z, by_near = {}, {}
    for p, span in enumerate(spans):
        for copy in by_y[p]:
            copy.wait_recv()
        total = part[y, :, span].astype(F32)
        for i in range(3):
            total += part_in[i, :, span].astype(F32)
        for k in range(Z):
            sums[k % 4 * CLASS + k // 4, :, span] = total[TOK * k : TOK * k + TOK, :].astype(BF16)
        cut = pl.ds(span.start, PIECES[p])
        if p >= len(PIECES) - DIRECT:
            by_z[p] = [
                send(
                    sums.at[chunk(lax.rem(z + dz, Z)), :, cut], sums_in.at[i, :, cut],
                    sums_s.at[p, i], sums_r.at[p, i], at(dz, 0),
                )
                for i, dz in enumerate(AROUND)
            ]
        else:
            by_near[p] = [
                send(
                    sums.at[pl.ds(lax.rem(low + dz, 4) * CLASS + first, count), :, cut],
                    near_in.at[i, pl.ds(first, count), :, cut],
                    part_near_s.at[p, j], part_near_r.at[p, j], at(dz, 0),
                )
                for j, (i, dz, first, count) in enumerate(
                    ((0, 1, 0, 4), (1, 15, 0, 4), (2, 2, 0, 2), (2, 14, 2, 2))
                )
            ]
        if p >= 1 and p - 1 in by_near:
            near_total(p - 1)
    if not DIRECT:
        near_total(len(PIECES) - 1)

    for copy in gather3:
        copy.wait_recv()
    tokens = gathered[...].reshape(256, columns)
    product = lax.dot_general(
        tokens, qt[...], (((1,), (1,)), ((), ())), preferred_element_type=F32
    )
    for k in range(Y * Z):
        start = k // Y % 4 * 64 + k % Y * 16 + k // 16 * TOK
        grad[k // 8, k % 8 * TOK : k % 8 * TOK + TOK, :] = product[start : start + TOK, :].astype(BF16)
    by_row = [
        send(
            grad.at[lax.rem(row + d, ROWS)], grad_in.at[d - 1],
            grad_s.at[d - 1], grad_r.at[d - 1], beside(d),
        )
        for d in range(1, ROWS)
    ]

    for c in range(0, columns, 256):
        block = gathered[:, :, c : c + 256].reshape(256, 256)
        product = lax.dot_general(
            block, x_by_class[...], (((0,), (0,)), ((), ())), preferred_element_type=F32
        )
        weight_ref[c : c + 256, :] = (product * (1.0 / math.sqrt(x_hbm.shape[0]))).astype(BF16)

    stores = [
        pltpu.make_async_copy(source, target, store_sem.at[i])
        for i, (source, target) in enumerate(
            ((weight_ref, weight_hbm), (input_ref, input_hbm), (projected_ref, projected_hbm))
        )
    ]
    stores[0].start()

    total = grad[row].astype(F32)
    for i, copy in enumerate(by_row):
        copy.wait_recv()
        total += grad_in[i].astype(F32)
    input_ref[...] = total.astype(BF16)
    stores[1].start()

    for p, span in enumerate(spans):
        direct = p >= len(PIECES) - DIRECT
        total = (sums[chunk(z), :, span] if direct else sums_far[high, :, span]).astype(F32)
        for i, copy in enumerate(by_z[p]):
            copy.wait_recv()
            total += sums_in[i, :, span].astype(F32)
        projected_ref[:, span] = total.astype(BF16)
    stores[2].start()

    for copy in near + far + gather1 + gather2 + gather3 + by_row + sum(by_y, []):
        copy.wait_send()
    for copy in sum(by_near.values(), []) + sum(by_z.values(), []):
        copy.wait_send()
    for copy in stores:
        copy.wait()


def hand_over(*refs):
    sources, targets, held, came, done = refs[:3], refs[3:6], refs[6:9], refs[9], refs[10]
    moves = []
    for source, target, here in zip(sources, targets, held):
        rows = source.shape[0]
        parts = 4 if rows >= 2048 else 1
        for k in range(parts):
            cut, i = pl.ds(k * (rows // parts), rows // parts), len(moves)
            moves.append((
                pltpu.make_async_copy(source.at[cut], here.at[cut], came.at[i]),
                pltpu.make_async_copy(here.at[cut], target.at[cut], done.at[i]),
            ))
    for come, _ in moves:
        come.start()
    for come, go in moves:
        come.wait()
        go.start()
    for _, go in moves:
        go.wait()


def local(inputs, weight, out_grad):
    columns, depth = weight.shape
    pieces = len(PIECES)
    anywhere = pl.BlockSpec(memory_space=pl.ANY)
    dma = pltpu.SemaphoreType.DMA
    results = pl.pallas_call(
        kernel,
        out_shape=(
            jax.ShapeDtypeStruct(out_grad.shape, BF16),
            jax.ShapeDtypeStruct((inputs.shape[0] // ROWS, depth), BF16),
            jax.ShapeDtypeStruct(weight.shape, BF16),
        ),
        in_specs=[anywhere] * 3,
        out_specs=(anywhere,) * 3,
        scratch_shapes=[
            pltpu.VMEM(out_grad.shape, BF16),
            pltpu.VMEM((inputs.shape[0] // ROWS, depth), BF16),
            pltpu.VMEM(weight.shape, BF16),
            dma((3,)),
            pltpu.VMEM(inputs.shape, BF16),
            pltpu.VMEM(weight.shape, BF16),
            pltpu.VMEM(out_grad.shape, BF16),
            dma((3,)),
            pltpu.VMEM((depth, columns), BF16),
            pltpu.VMEM((depth, columns), BF16),
            pltpu.VMEM((Y * Z, TOK, columns), BF16),
            pltpu.VMEM(inputs.shape, BF16),
            pltpu.VMEM(inputs.shape, BF16),
            pltpu.VMEM((2, columns // 2), BF16),
            pltpu.VMEM((len(WINDOW), 2, columns // 2), BF16),
            pltpu.VMEM((2, columns // 2), BF16),
            pltpu.VMEM((len(FAR), 2, columns // 2), BF16),
            pltpu.VMEM((Y, Z * TOK, columns), BF16),
            pltpu.VMEM((Y - 1, Z * TOK, columns), BF16),
            pltpu.VMEM((Z, TOK, columns), BF16),
            pltpu.VMEM((3, CLASS, TOK, columns), BF16),
            pltpu.VMEM((CLASS, TOK, columns), BF16),
            pltpu.VMEM((Z - 1, TOK, columns), BF16),
            pltpu.VMEM((ROWS, inputs.shape[0] // ROWS, depth), BF16),
            pltpu.VMEM((ROWS - 1, inputs.shape[0] // ROWS, depth), BF16),
            dma((len(WINDOW),)), dma((len(WINDOW),)), dma((len(FAR),)), dma((len(FAR),)),
            dma((len(FAR),)), dma((len(FAR),)), dma((6,)), dma((6,)), dma((21,)), dma((21,)),
            dma((pieces, Y - 1)), dma((pieces, Y - 1)), dma((pieces, 4)), dma((pieces, 4)),
            dma((pieces, Z - 1)), dma((pieces, Z - 1)),
            dma((ROWS - 1,)), dma((ROWS - 1,)),
        ],
        compiler_params=pltpu.CompilerParams(
            collective_id=0, has_side_effects=True, vmem_limit_bytes=56 * 2**20
        ),
        name="joined_projection",
    )(inputs, weight, out_grad)
    return pl.pallas_call(
        hand_over,
        out_shape=tuple(jax.ShapeDtypeStruct(a.shape, a.dtype) for a in results),
        in_specs=[anywhere] * 3,
        out_specs=(anywhere,) * 3,
        scratch_shapes=[pltpu.VMEM(a.shape, a.dtype) for a in results] + [dma((6,)), dma((6,))],
        name="hand_over",
    )(*results)


def solution(mesh):
    placed = (P(None, "ka"), P("row", "ka"), P("ka", "row"))
    return jax.shard_map(
        local,
        mesh=mesh,
        in_specs=placed,
        out_specs=(P("ka", "row"), P("row", "ka"), P("row", "ka")),
        check_vma=False,
    )
```
